32 devices in a mesh: dp: 8 (over z, x), expert: 4 (over y, core).
Axes of the slice: x: 2, y: 2, z: 4, core: 2. Of those that a mesh axis runs over, the one named last changes fastest.
Arguments:
- tokens: bfloat16 [32, 4096], P(('dp', 'expert')), may hold values from -6 to 6
- cotangent: bfloat16 [32, 4096], P(('dp', 'expert')), may hold values from -1.5 to 1.5
- route_ids: int32 [32, 2], replicated, may hold values from 0 to 3, all different within a row; in each aligned block of 4 rows (0 to 3, 4 to 7, ...) at most 4 rows name the same one
- w_router: bfloat16 [4, 4096], replicated, may hold values from -0.09375 to 0.09375
- w_up: bfloat16 [4, 4096, 8192], P('expert', None, 'dp'), may hold values from -0.09375 to 0.09375
- down_weight: bfloat16 [4, 8192, 4096], P('expert', 'dp'), may hold values from -0.0625 to 0.0625
Outputs:
- grad_up: bfloat16 [4, 4096, 8192], P('expert', None, 'dp')
- grad_down: bfloat16 [4, 8192, 4096], P('expert', 'dp')
- grad_router: float32 [4, 4096], replicated
The draws below stay inside these ranges and needn't reach their ends.
Inputs may be any that keep to these rules, and one draw needn't show every extreme that they name: `route_ids`: the two ids of a token differ. Within the tokens of one dp index (aligned blocks of 4 rows) no expert is named more than 4 times, a bound that some block reaches.
All inputs are finite; a program needn't handle non-finite values.
Results may differ from the reference program's by a relative error of at most 0.0058.
Values may be sent and summed in bfloat16 or wider, within the bound.
No kernel may reach another device: no remote copies, remote signals or barrier semaphores. Data moves between devices by JAX's collectives and lax.ppermute only.
A program may use at most 128 MiB of HBM per device.

```python
import math
import jax
import jax.numpy as jnp
import numpy as np
from jax import lax

MODEL_WIDTH = 4096
FF = 8192
EXPERTS = 4
TOKENS = 32
BLOCK = 4
MOST = 4
EXPERT_ROWS = 32


def steps_of(stream_key, extent, split, smallest, largest):
    level = 1.0
    for position, shards_of in split:
        steps = jax.random.uniform(jax.random.fold_in(jax.random.fold_in(stream_key, 6), position), (shards_of,), jnp.float32, smallest / len(split), largest / len(split))
        level = level * jnp.repeat(jnp.exp(steps), extent[position] // shards_of).reshape((-1,) + (1,) * (len(extent) - 1 - position))
    return level


def routed_block(stream_key, own, number, rows, number_of, top, limit, skew):
    sequence = jax.random.permutation(stream_key, number_of)
    heavy_load, usual = load_shares(number_of, rows * top, limit, skew, True), load_shares(number_of, rows * top, limit, skew, False)
    places = jnp.arange(number_of)

    def named(sizes, offset_by):
        used = int((sizes > 0).sum())
        fixed = max(1, used // 4)
        passed = fixed + (places - fixed + offset_by * (used - fixed)) % max(1, number_of - fixed)
        return jnp.zeros((number_of,), jnp.int32).at[sequence[jnp.where(places < fixed, places, passed)]].set(jnp.asarray(sizes, jnp.int32))

    sizes = jnp.where(number % 4 == 0, named(heavy_load, number // 4), named(usual, number - number // 4 - 1))
    mixed = jax.random.permutation(jax.random.fold_in(own, 3), number_of)
    giver, taker = mixed[0:number_of // 2 * 2:2], mixed[1:number_of // 2 * 2:2]
    margin = jnp.minimum(sizes[giver] - 1, limit - sizes[taker]) // 2
    margin = jnp.where((giver == sequence[0]) | (taker == sequence[0]) | (sizes[taker] == 0), 0, jnp.maximum(margin, 0))
    passed = jax.random.randint(jax.random.fold_in(own, 4), (number_of // 2,), 0, 1 << 20) % (margin + 1)
    sizes = sizes.at[giver].add(-passed).at[taker].add(passed)
    members = jnp.searchsorted(jnp.cumsum(sizes), jnp.arange(rows * top), side="right").astype(jnp.int32)
    listing = members.reshape(top, rows).T
    listing = listing[jax.random.permutation(jax.random.fold_in(own, 1), rows)]
    offset_by = jax.random.randint(jax.random.fold_in(own, 2), (rows, 1), 0, top)
    return jnp.take_along_axis(listing, (jnp.arange(top)[None, :] + offset_by) % top, axis=1)


def load_shares(number_of, total, limit, slope, full):
    loads = [(1 << 20) // math.isqrt(grade ** slope) + 1 for grade in range(1, number_of + 1)]
    largest = limit if full else min(limit, max(-(-total // number_of), total * loads[0] // sum(loads)))
    least = 1 if total - largest >= number_of - 1 else 0
    given, surplus = [largest] + [least] * (number_of - 1), total - largest - least * (number_of - 1)
    while surplus > 0:
        free = [i for i in range(1, number_of) if given[i] < largest] or [i for i in range(1, number_of) if given[i] < limit]
        mass, remaining = sum([loads[i] for i in free]), surplus
        for i in free:
            extra = min(limit - given[i], max(1, remaining * loads[i] // mass), surplus)
            given[i] = given[i] + extra
            surplus = surplus - extra
    return np.array(given)


def scatter_about(rng, shape, width, bound, pieces=(), held_as=jnp.bfloat16):
    values = jax.random.normal(rng, shape, jnp.float32) * width
    if len(pieces) > 0:
        values = steps_of(rng, shape, pieces, -0.22, 0.18) * values
    return jnp.clip(values, min=-bound, max=bound).astype(held_as)


def setup_inputs(seed: int = 0) -> dict:
    arg_keys = jax.random.split(jax.random.key(seed), 7)
    tokens = scatter_about(arg_keys[0], (TOKENS, MODEL_WIDTH), 1.0, 6.0, ((0, 32),))
    cotangent = scatter_about(arg_keys[1], (TOKENS, MODEL_WIDTH), 0.25, 1.5, ((0, 32),))
    route_ids_keys = jax.random.split(jax.random.fold_in(arg_keys[2], 1), TOKENS // BLOCK)
    route_ids_turns = jax.random.permutation(jax.random.fold_in(arg_keys[2], 3), TOKENS // BLOCK)
    route_ids = jax.vmap(lambda own, number: routed_block(jax.random.fold_in(arg_keys[2], 2), own, number, BLOCK, EXPERTS, 2, MOST, 2))(route_ids_keys, route_ids_turns).reshape((TOKENS, 2))
    w_router = scatter_about(arg_keys[3], (EXPERTS, MODEL_WIDTH), MODEL_WIDTH ** -0.5, 0.09375)
    w_up = scatter_about(arg_keys[4], (EXPERTS, MODEL_WIDTH, FF), MODEL_WIDTH ** -0.5, 0.09375, ((0, 4), (2, 8)))
    down_weight = scatter_about(arg_keys[5], (EXPERTS, FF, MODEL_WIDTH), FF ** -0.5, 0.0625, ((0, 4), (1, 8)))
    return {"tokens": tokens, "cotangent": cotangent, "route_ids": route_ids, "w_router": w_router, "w_up": w_up, "down_weight": down_weight}


def reference(tokens, cotangent, route_ids, w_router, w_up, down_weight):
    logits = jnp.dot(tokens, w_router.T, preferred_element_type=jnp.float32)
    columns = jnp.arange(EXPERTS, dtype=jnp.int32)
    first_mask = route_ids[:, 0:1] == columns[None, :]
    second_mask = route_ids[:, 1:2] == columns[None, :]
    logit_first = jnp.sum(jnp.where(first_mask, logits, 0.0), axis=1)
    logit_second = jnp.sum(jnp.where(second_mask, logits, 0.0), axis=1)
    p_first = jax.nn.sigmoid(logit_first - logit_second)
    p_second = jax.nn.sigmoid(logit_second - logit_first)
    token_index = jnp.arange(TOKENS, dtype=jnp.int32)
    block_of = token_index // BLOCK
    q_first = jnp.zeros((TOKENS,), jnp.float32)
    q_second = jnp.zeros((TOKENS,), jnp.float32)
    ups = []
    down_outputs = []
    for expert_number in range(EXPERTS):
        is_first = first_mask[:, expert_number]
        is_second = second_mask[:, expert_number]
        routed = is_first | is_second
        weight = jnp.where(is_first, p_first, 0.0) + jnp.where(is_second, p_second, 0.0)
        ranks = jnp.cumsum(routed.astype(jnp.int32).reshape(TOKENS // BLOCK, BLOCK), axis=1).reshape(TOKENS) - 1
        buffer_rows = jnp.where(routed, block_of * MOST + ranks, EXPERT_ROWS).astype(jnp.int32)
        xbuf = jnp.zeros((EXPERT_ROWS, MODEL_WIDTH), jnp.bfloat16).at[buffer_rows].set(tokens, mode="drop")
        gradient_values = (weight[:, None] * cotangent.astype(jnp.float32)).astype(jnp.bfloat16)
        gradient_buffer = jnp.zeros((EXPERT_ROWS, MODEL_WIDTH), jnp.bfloat16).at[buffer_rows].set(gradient_values, mode="drop")
        pre_act = jnp.dot(xbuf, w_up[expert_number], preferred_element_type=jnp.float32)
        returned_gradient = jnp.dot(gradient_buffer, down_weight[expert_number].T, preferred_element_type=jnp.float32)
        sig_pre = jax.nn.sigmoid(pre_act)
        silu_act = pre_act * sig_pre
        row_sums = jnp.sum(silu_act * returned_gradient, axis=1)
        hidden_state = silu_act.astype(jnp.bfloat16)
        pre_grad = (returned_gradient * sig_pre * (1.0 + pre_act * (1.0 - sig_pre))).astype(jnp.bfloat16)
        down_outputs.append(jnp.dot(hidden_state.T, gradient_buffer, preferred_element_type=jnp.float32).astype(jnp.bfloat16))
        ups.append(jnp.dot(xbuf.T, pre_grad, preferred_element_type=jnp.float32).astype(jnp.bfloat16))
        token_sums = jnp.take(row_sums, jnp.minimum(buffer_rows, EXPERT_ROWS - 1).astype(jnp.int32))
        q_first = q_first + jnp.where(is_first, token_sums, 0.0)
        q_second = q_second + jnp.where(is_second, token_sums, 0.0)
    delta = p_second * q_first - p_first * q_second
    dlogit = jnp.where(first_mask, delta[:, None], 0.0) - jnp.where(second_mask, delta[:, None], 0.0)
    grad_router = jnp.dot(dlogit.T, tokens.astype(jnp.float32), precision=lax.Precision.HIGHEST)
    return jnp.stack(ups), jnp.stack(down_outputs), grad_router
```

```python
import functools

import jax
import jax.numpy as jnp
from jax import lax
from jax.experimental import pallas as pl
from jax.experimental.pallas import tpu as pltpu
from jax.sharding import PartitionSpec as P

F32 = jnp.float32
BF16 = jnp.bfloat16
AXES = ("dp", "expert")
VMEM_LIMIT = 56 * 1024 * 1024


def gather_rows(row, n):
    order = [0]
    bit = n // 2
    while bit:
        other = lax.ppermute(row, AXES, [(i, i ^ bit) for i in range(n)])
        row = jnp.concatenate([row, other], axis=0)
        order = order + [o ^ bit for o in order]
        bit //= 2
    return row, order


def one_hot(row_tok, rows):
    return row_tok == lax.broadcasted_iota(jnp.int32, (rows, rows), 1)


def forward_kernel(
    who, row_tok, ids, w_router, xg, w_up, down, hidden, dpre, gs, terms, up_buf, down_buf, sems
):
    rows = xg.shape[0]
    width = w_up.shape[0]
    ff = w_up.shape[1]
    chunks = sems.shape[1]
    kc = width // chunks
    fc = ff // chunks
    ups = [
        pltpu.make_async_copy(w_up.at[pl.ds(i * kc, kc)], up_buf.at[pl.ds(i * kc, kc)], sems.at[0, i])
        for i in range(chunks)
    ]
    downs = [
        pltpu.make_async_copy(down.at[pl.ds(i * fc, fc)], down_buf.at[pl.ds(i * fc, fc)], sems.at[1, i])
        for i in range(chunks)
    ]
    for c in ups + downs:
        c.start()
    expert = who[0, 0]
    perm = one_hot(row_tok[...], rows)
    pair = jnp.dot(
        perm.astype(BF16), ids[...].astype(F32).astype(BF16), preferred_element_type=F32
    ).astype(jnp.int32)
    logits = lax.dot_general(
        xg[:, :width], w_router[...], (((1,), (1,)), ((), ())), preferred_element_type=F32
    )
    columns = lax.broadcasted_iota(jnp.int32, logits.shape, 1)
    first = pair[:, 0:1]
    second = pair[:, 1:2]
    l0 = jnp.sum(jnp.where(first == columns, logits, 0.0), axis=1, keepdims=True)
    l1 = jnp.sum(jnp.where(second == columns, logits, 0.0), axis=1, keepdims=True)
    p0 = jax.nn.sigmoid(l0 - l1)
    p1 = jax.nn.sigmoid(l1 - l0)
    is0 = first == expert
    is1 = second == expert
    weight = jnp.where(is0, p0, 0.0) + jnp.where(is1, p1, 0.0)
    gs[...] = (weight * xg[:, width:].astype(F32)).astype(BF16)
    pre = jnp.zeros((rows, ff), F32)
    for i in range(chunks):
        ups[i].wait()
        pre = pre + jnp.dot(
            xg[:, i * kc : (i + 1) * kc], up_buf[i * kc : (i + 1) * kc, :], preferred_element_type=F32
        )
    sig = jax.nn.sigmoid(pre)
    silu = pre * sig
    slope = sig * (1.0 + pre * (1.0 - sig))
    hidden[...] = silu.astype(BF16)
    q = jnp.zeros((rows, 1), F32)
    for i in range(chunks):
        downs[i].wait()
        back = lax.dot_general(
            gs[...],
            down_buf[i * fc : (i + 1) * fc, :],
            (((1,), (1,)), ((), ())),
            preferred_element_type=F32,
        )
        part = slice(i * fc, (i + 1) * fc)
        q = q + jnp.sum(silu[:, part] * back, axis=1, keepdims=True)
        dpre[:, part] = (back * slope[:, part]).astype(BF16)
    dl = (jnp.where(is0, p1, 0.0) - jnp.where(is1, p0, 0.0)) * q
    line = jnp.sum(jnp.where(perm, dl, 0.0), axis=0, keepdims=True)
    terms[...] = jnp.broadcast_to(line[None], terms.shape)


def forward(who, row_tok, ids, w_router, xg, w_up, down, n):
    rows = xg.shape[0]
    width, ff = w_up.shape
    chunks = 8 if ff % 1024 == 0 else 1
    vm = pl.BlockSpec(memory_space=pltpu.VMEM)
    hbm = pl.BlockSpec(memory_space=pltpu.HBM)
    return pl.pallas_call(
        forward_kernel,
        out_shape=(
            jax.ShapeDtypeStruct((rows, ff), BF16),
            jax.ShapeDtypeStruct((rows, ff), BF16),
            jax.ShapeDtypeStruct((rows, width), BF16),
            jax.ShapeDtypeStruct((n, 1, rows), F32),
        ),
        in_specs=[pl.BlockSpec(memory_space=pltpu.SMEM), vm, vm, vm, vm, hbm, hbm],
        out_specs=(vm, vm, vm, vm),
        scratch_shapes=[
            pltpu.VMEM(w_up.shape, BF16),
            pltpu.VMEM(down.shape, BF16),
            pltpu.SemaphoreType.DMA((2, chunks)),
        ],
        compiler_params=pltpu.CompilerParams(vmem_limit_bytes=VMEM_LIMIT),
        name="forward",
    )(who, row_tok, ids, w_router, xg, w_up, down)


def grads_kernel(x, hidden, dpre, gs, up_out, down_out):
    up_out[...] = lax.dot_general(
        x[...], dpre[...], (((0,), (0,)), ((), ())), preferred_element_type=F32
    ).astype(BF16)
    down_out[...] = lax.dot_general(
        hidden[...], gs[...], (((0,), (0,)), ((), ())), preferred_element_type=F32
    ).astype(BF16)


def grads(xg, hidden, dpre, gs):
    rows, ff = hidden.shape
    width = gs.shape[1]
    steps = 8 if ff % 1024 == 0 else 1
    kc, fc = width // steps, ff // steps
    return pl.pallas_call(
        grads_kernel,
        grid=(steps,),
        out_shape=(
            jax.ShapeDtypeStruct((width, ff), BF16),
            jax.ShapeDtypeStruct((ff, width), BF16),
        ),
        in_specs=[
            pl.BlockSpec((rows, kc), lambda i: (0, i)),
            pl.BlockSpec((rows, fc), lambda i: (0, i)),
            pl.BlockSpec((rows, ff), lambda i: (0, 0)),
            pl.BlockSpec((rows, width), lambda i: (0, 0)),
        ],
        out_specs=(
            pl.BlockSpec((kc, ff), lambda i: (i, 0)),
            pl.BlockSpec((fc, width), lambda i: (i, 0)),
        ),
        compiler_params=pltpu.CompilerParams(vmem_limit_bytes=VMEM_LIMIT),
        name="grads",
    )(xg, hidden, dpre, gs)


def router_kernel(terms, row_tok, ids, xg, out):
    rows = xg.shape[0]
    width = out.shape[1]
    dl = jnp.sum(terms[...], axis=0)
    perm = one_hot(row_tok[...], rows).astype(BF16)
    x = lax.dot_general(
        perm, xg[:, :width], (((0,), (0,)), ((), ())), preferred_element_type=F32
    ).astype(BF16)
    experts = lax.broadcasted_iota(jnp.int32, (out.shape[0], rows), 0)
    dlogit = jnp.where(ids[0:1, :] == experts, dl, 0.0) - jnp.where(ids[1:2, :] == experts, dl, 0.0)
    high = dlogit.astype(BF16)
    rest = dlogit - high.astype(F32)
    mid = rest.astype(BF16)
    low = (rest - mid.astype(F32)).astype(BF16)
    dot = functools.partial(jnp.dot, preferred_element_type=F32)
    out[...] = dot(low, x) + dot(mid, x) + dot(high, x)


def router(terms, row_tok, ids_t, xg, n_experts, width):
    vm = pl.BlockSpec(memory_space=pltpu.VMEM)
    return pl.pallas_call(
        router_kernel,
        out_shape=jax.ShapeDtypeStruct((n_experts, width), F32),
        in_specs=[vm] * 4,
        out_specs=vm,
        compiler_params=pltpu.CompilerParams(vmem_limit_bytes=VMEM_LIMIT),
        name="router",
    )(terms, row_tok, ids_t, xg)


def local(tokens, cotangent, route_ids, w_router, w_up, down_weight):
    n = lax.axis_size("dp") * lax.axis_size("expert")
    me = lax.axis_index("dp") * lax.axis_size("expert") + lax.axis_index("expert")
    who = lax.axis_index("expert").astype(jnp.int32).reshape(1, 1)
    xg, order = gather_rows(jnp.concatenate([tokens, cotangent], axis=1), n)
    row_tok = (jnp.asarray(order, jnp.int32) ^ me).reshape(n, 1)
    hidden, dpre, gs, terms = forward(
        who, row_tok, route_ids, w_router, xg, w_up[0], down_weight[0], n
    )
    terms = lax.all_to_all(terms, AXES, 0, 0, tiled=True)
    grad_up, grad_down = grads(xg, hidden, dpre, gs)
    grad_router = router(terms, row_tok, route_ids.T, xg, w_router.shape[0], tokens.shape[1])
    return (grad_up[None], grad_down[None], grad_router)


def solution(mesh):
    return jax.shard_map(
        local,
        mesh=mesh,
        in_specs=(
            P(AXES, None),
            P(AXES, None),
            P(),
            P(),
            P("expert", None, "dp"),
            P("expert", "dp", None),
        ),
        out_specs=(P("expert", None, "dp"), P("expert", "dp", None), P()),
        check_vma=False,
    )
```

```python
import functools

import jax
import jax.numpy as jnp
from jax import lax
from jax.experimental import pallas as pl
from jax.experimental.pallas import tpu as pltpu
from jax.sharding import Mesh, PartitionSpec as P

F32 = jnp.float32
BF16 = jnp.bfloat16
CHIPS = ("dp", "ey")
AXES = ("dp", "ey", "core")
MIB = 1024 * 1024
VM = pl.BlockSpec(memory_space=pltpu.VMEM)
HBM = pl.BlockSpec(memory_space=pltpu.HBM)


def dot(a, b, ca=1, cb=0):
    return lax.dot_general(a, b, (((ca,), (cb,)), ((), ())), preferred_element_type=F32)


def in_hbm(x):
    return pltpu.with_memory_space_constraint(x, pltpu.HBM)


def pack_kernel(tokens, cotangent, out, buf, sems):
    loads = [
        pltpu.make_async_copy(ref, buf.at[i], sems.at[i]) for i, ref in enumerate((tokens, cotangent))
    ]
    for c in loads:
        c.start()
    for c in loads:
        c.wait()
    both = jnp.concatenate([buf[0], buf[1]], axis=0)
    out[...] = jnp.broadcast_to(both[None], out.shape)


def pack(tokens, cotangent, n):
    return pl.pallas_call(
        pack_kernel,
        out_shape=pltpu.VMEM((n, 2, tokens.shape[1]), BF16),
        in_specs=[HBM, HBM],
        out_specs=VM,
        scratch_shapes=[pltpu.VMEM((2,) + tokens.shape, BF16), pltpu.SemaphoreType.DMA((2,))],
        compiler_params=pltpu.CompilerParams(vmem_limit_bytes=16 * MIB),
        name="pack",
    )(in_hbm(tokens), in_hbm(cotangent))


def token_of_row(rows, core, shape, dim):
    row = lax.broadcasted_iota(jnp.int32, shape, dim)
    half = rows // 2
    return jnp.where(row < half, 2 * row + core, 2 * (row - half) + 1 - core)


def forward_kernel(
    chunks,
    ids_in,
    gate_in,
    mine,
    other,
    w_up,
    down,
    x,
    gs,
    hidden,
    dpre,
    terms,
    ids,
    gate,
    up_buf,
    down_buf,
    sems,
):
    rows, width = x.shape
    kc = width // chunks
    half = rows // 2
    small = [
        pltpu.make_async_copy(gate_in, gate, sems.at[2, 0]),
        pltpu.make_async_copy(ids_in, ids, sems.at[2, 1]),
    ]
    ups, downs = [], []
    for i in range(chunks):
        part = pl.ds(i * kc, kc)
        downs.append(pltpu.make_async_copy(down.at[:, part], down_buf.at[:, part], sems.at[0, i]))
        ups.append(pltpu.make_async_copy(w_up.at[part], up_buf.at[part], sems.at[1, i]))
    for c in small + downs + ups:
        c.start()
    expert = 2 * lax.axis_index("ey") + lax.axis_index("core")
    core = lax.axis_index("core")
    x[:half, :] = mine[:, 0, :]
    x[half:, :] = other[:, 0, :]
    for c in small:
        c.wait()
    place = lax.broadcasted_iota(jnp.int32, (rows, rows), 1)
    perm = token_of_row(rows, core, (rows, rows), 0) == place
    first = jnp.sum(jnp.where(perm, ids[0:1, :], 0), axis=1, keepdims=True)
    second = jnp.sum(jnp.where(perm, ids[1:2, :], 0), axis=1, keepdims=True)
    logits = dot(x[...], gate[...], 1, 1)
    columns = lax.broadcasted_iota(jnp.int32, logits.shape, 1)
    l0 = jnp.sum(jnp.where(first == columns, logits, 0.0), axis=1, keepdims=True)
    l1 = jnp.sum(jnp.where(second == columns, logits, 0.0), axis=1, keepdims=True)
    p0 = jax.nn.sigmoid(l0 - l1)
    p1 = jax.nn.sigmoid(l1 - l0)
    is0 = first == expert
    is1 = second == expert
    weight = jnp.where(is0, p0, 0.0) + jnp.where(is1, p1, 0.0)
    gs[:half, :] = (weight[:half] * mine[:, 1, :].astype(F32)).astype(BF16)
    gs[half:, :] = (weight[half:] * other[:, 1, :].astype(F32)).astype(BF16)
    back = None
    for i in range(chunks):
        downs[i].wait()
        part = slice(i * kc, (i + 1) * kc)
        term = dot(gs[:, part], down_buf[:, part], 1, 1)
        back = term if back is None else back + term
    pre = None
    for i in range(chunks):
        ups[i].wait()
        part = slice(i * kc, (i + 1) * kc)
        term = dot(x[:, part], up_buf[part, :])
        pre = term if pre is None else pre + term
    sig = jax.nn.sigmoid(pre)
    silu = pre * sig
    hidden[...] = silu.astype(BF16)
    dpre[...] = (back * sig * (1.0 + pre * (1.0 - sig))).astype(BF16)
    q = jnp.sum(silu * back, axis=1, keepdims=True)
    dl = (jnp.where(is0, p1, 0.0) - jnp.where(is1, p0, 0.0)) * q
    line = jnp.sum(jnp.where(perm, dl, 0.0), axis=0, keepdims=True)
    terms[...] = jnp.broadcast_to(line[None], terms.shape)


def forward(ids, w_router, mine, other, w_up, down):
    rows = 2 * mine.shape[0]
    width, ff = w_up.shape
    chunks = 8
    return pl.pallas_call(
        functools.partial(forward_kernel, chunks),
        out_shape=(
            pltpu.VMEM((rows, width), BF16),
            pltpu.VMEM((rows, width), BF16),
            pltpu.VMEM((rows, ff), BF16),
            pltpu.VMEM((rows, ff), BF16),
            pltpu.VMEM((rows, 1, rows), F32),
        ),
        in_specs=[HBM] * 2 + [VM] * 2 + [HBM] * 2,
        out_specs=(VM,) * 5,
        scratch_shapes=[
            pltpu.VMEM(ids.shape, jnp.int32),
            pltpu.VMEM(w_router.shape, BF16),
            pltpu.VMEM(w_up.shape, BF16),
            pltpu.VMEM(down.shape, BF16),
            pltpu.SemaphoreType.DMA((3, chunks)),
        ],
        compiler_params=pltpu.CompilerParams(vmem_limit_bytes=40 * MIB),
        name="forward",
    )(in_hbm(ids), in_hbm(w_router), mine, other, in_hbm(w_up), in_hbm(down))


def grads_kernel(
    chunks, x, gs, hidden, dpre, up_out, down_out, up_buf, down_buf, sems
):
    rows, width = x.shape
    ff = hidden.shape[1]
    kc, fc = width // chunks, ff // chunks
    copies = []
    for i in range(chunks):
        part = slice(i * fc, (i + 1) * fc)
        down_buf[part, :] = dot(hidden[:, part], gs[...], 0, 0).astype(BF16)
        copies.append(pltpu.make_async_copy(down_buf.at[part], down_out.at[part], sems.at[0, i]))
        copies[-1].start()
        part = slice(i * kc, (i + 1) * kc)
        up_buf[part, :] = dot(x[:, part], dpre[...], 0, 0).astype(BF16)
        copies.append(pltpu.make_async_copy(up_buf.at[part], up_out.at[part], sems.at[1, i]))
        copies[-1].start()
    for c in copies:
        c.wait()


def grads(x, gs, hidden, dpre):
    rows, width = x.shape
    ff = hidden.shape[1]
    chunks = 8 if ff % 1024 == 0 else 1
    return pl.pallas_call(
        functools.partial(grads_kernel, chunks),
        out_shape=(
            jax.ShapeDtypeStruct((width, ff), BF16),
            jax.ShapeDtypeStruct((ff, width), BF16),
        ),
        in_specs=[VM] * 4,
        out_specs=(HBM, HBM),
        scratch_shapes=[
            pltpu.VMEM((width, ff), BF16),
            pltpu.VMEM((ff, width), BF16),
            pltpu.SemaphoreType.DMA((2, chunks)),
        ],
        compiler_params=pltpu.CompilerParams(vmem_limit_bytes=40 * MIB),
        name="grads",
    )(x, gs, hidden, dpre)


def router_kernel(ids, x, terms, router_out):
    rows = x.shape[0]
    half = rows // 2
    core = lax.axis_index("core")
    dl = jnp.sum(terms[...], axis=0)
    experts = router_out.shape[0]
    expert = lax.broadcasted_iota(jnp.int32, (experts, rows), 0)
    dlogit = jnp.where(ids[0:1, :] == expert, dl, 0.0) - jnp.where(ids[1:2, :] == expert, dl, 0.0)
    high = dlogit.astype(BF16)
    rest = dlogit - high.astype(F32)
    mid = rest.astype(BF16)
    low = (rest - mid.astype(F32)).astype(BF16)
    perm = token_of_row(rows, core, (rows, rows), 1) == lax.broadcasted_iota(jnp.int32, (rows, rows), 0)
    split = dot(jnp.concatenate([low, mid, high], axis=0), perm.astype(BF16)).astype(BF16)
    sums = []
    for part in (slice(0, half), slice(half, rows)):
        s = dot(split[:, part], x[part, :])
        sums.append(s[:experts] + s[experts : 2 * experts] + s[2 * experts :])
    router_out[...] = sums[0] + sums[1]


def router(ids, x, terms, experts):
    return pl.pallas_call(
        router_kernel,
        out_shape=jax.ShapeDtypeStruct((experts, x.shape[1]), F32),
        in_specs=[VM] * 3,
        out_specs=VM,
        compiler_params=pltpu.CompilerParams(vmem_limit_bytes=16 * MIB),
        name="router",
    )(ids, x, terms)


def local(tokens, cotangent, route_ids, w_router, w_up, down_weight):
    chips = lax.axis_size("dp") * lax.axis_size("ey")
    ids = route_ids.T
    mine = lax.all_to_all(pack(tokens, cotangent, chips), CHIPS, 0, 0, tiled=True)
    other = lax.ppermute(mine, "core", [(0, 1), (1, 0)])
    x, gs, hidden, dpre, terms = forward(ids, w_router, mine, other, w_up[0], down_weight[0])
    terms = lax.all_to_all(terms, AXES, 0, 0, tiled=True)
    grad_up, grad_down = grads(x, gs, hidden, dpre)
    grad_router = router(ids, x, terms, w_router.shape[0])
    return (grad_up[None], grad_down[None], grad_router)


def solution(mesh):
    n_data, n_experts = mesh.shape["dp"], mesh.shape["expert"]
    split = Mesh(mesh.devices.reshape(n_data, n_experts // 2, 2), AXES)
    experts = ("ey", "core")
    return jax.shard_map(
        local,
        mesh=split,
        in_specs=(
            P(AXES, None),
            P(AXES, None),
            P(),
            P(),
            P(experts, None, "dp"),
            P(experts, "dp", None),
        ),
        out_specs=(P(experts, None, "dp"), P(experts, "dp", None), P()),
        check_vma=False,
    )
```

```python
import functools

import jax
import jax.numpy as jnp
from jax import lax
from jax.experimental import pallas as pl
from jax.experimental.pallas import tpu as pltpu
from jax.sharding import Mesh, PartitionSpec as P

F32 = jnp.float32
BF16 = jnp.bfloat16
CHIPS = ("dp", "ey")
AXES = ("dp", "ey", "core")
MIB = 1024 * 1024
VM = pl.BlockSpec(memory_space=pltpu.VMEM)
HBM = pl.BlockSpec(memory_space=pltpu.HBM)


def dot(a, b, ca=1, cb=0):
    return lax.dot_general(a, b, (((ca,), (cb,)), ((), ())), preferred_element_type=F32)


def in_hbm(x):
    return pltpu.with_memory_space_constraint(x, pltpu.HBM)


def pack_kernel(tokens, cotangent, out, buf, sems):
    loads = [
        pltpu.make_async_copy(ref, buf.at[i], sems.at[i]) for i, ref in enumerate((tokens, cotangent))
    ]
    for c in loads:
        c.start()
    for c in loads:
        c.wait()
    out[...] = jnp.concatenate([buf[0], buf[1]], axis=0)[None]


def pack(tokens, cotangent):
    return pl.pallas_call(
        pack_kernel,
        out_shape=pltpu.VMEM((1, 2, tokens.shape[1]), BF16),
        in_specs=[HBM, HBM],
        out_specs=VM,
        scratch_shapes=[pltpu.VMEM((2,) + tokens.shape, BF16), pltpu.SemaphoreType.DMA((2,))],
        compiler_params=pltpu.CompilerParams(vmem_limit_bytes=16 * MIB),
        name="pack",
    )(in_hbm(tokens), in_hbm(cotangent))


def stages(n):
    bits = n.bit_length() - 1
    shifts, high = [], bits
    while high > 1:
        low = max(1, high - 2)
        shifts.append((low, high - low))
        high = low
    return shifts


def spread(blocks, n, shift, count):
    parts = [blocks]
    for step in range(1, 1 << count):
        pairs = [(i, i ^ (step << shift)) for i in range(n)]
        parts.append(lax.ppermute(blocks, AXES, pairs))
    return jnp.concatenate(parts, axis=0)


def prefetch_kernel(count, *refs):
    sources, targets, sems = refs[:count], refs[-1 - count : -1], refs[-1]
    copies = [
        pltpu.make_async_copy(source, target, sems.at[i])
        for i, (source, target) in enumerate(zip(sources, targets))
    ]
    for c in copies:
        c.start()
    if len(refs) > 2 * count + 1:
        held, turned = refs[count], refs[count + 1]
        step = min(256, held.shape[0])
        for i in range(0, held.shape[0], step):
            turned[:, i : i + step] = held[i : i + step, :].T
    for c in copies:
        c.wait()


def prefetch(arrays, held=None):
    extra = [] if held is None else [held]
    turned = [pltpu.VMEM(h.shape[::-1], h.dtype) for h in extra]
    return pl.pallas_call(
        functools.partial(prefetch_kernel, len(arrays)),
        out_shape=tuple(turned) + tuple(pltpu.VMEM(a.shape, a.dtype) for a in arrays),
        in_specs=[HBM] * len(arrays) + [VM] * len(extra),
        out_specs=(VM,) * (len(arrays) + len(extra)),
        scratch_shapes=[pltpu.SemaphoreType.DMA((len(arrays),))],
        compiler_params=pltpu.CompilerParams(vmem_limit_bytes=8 * MIB),
        name="turn" if extra else "prefetch",
    )(*[in_hbm(a) for a in arrays], *extra)


def device_index():
    place = lax.axis_index("dp") * lax.axis_size("ey") + lax.axis_index("ey")
    return 2 * place + lax.axis_index("core")


def token_of_row(rows, shape, dim):
    row = lax.broadcasted_iota(jnp.int32, shape, dim)
    half = rows // 2
    token = jnp.where(row < half, 0, 1) ^ device_index()
    digits = lax.rem(row, half)
    for shift, count in stages(rows):
        token = token ^ ((digits & ((1 << count) - 1)) << shift)
        digits = digits >> count
    return token


def row_dots(x, gate):
    if x.shape[0] > 64:
        return dot(x[...], gate[...], 1, 1)
    sums = []
    for e in range(gate.shape[0]):
        total = jnp.zeros((x.shape[0], 128), F32)
        for k in range(0, x.shape[1], 128):
            part = slice(k, k + 128)
            total = total + x[:, part].astype(F32) * gate[e : e + 1, part].astype(F32)
        sums.append(jnp.sum(total, axis=1, keepdims=True))
    return jnp.concatenate(sums, axis=1)


def gate_values(ids, gate, x):
    rows = x.shape[0]
    place = lax.broadcasted_iota(jnp.int32, (rows, rows), 1)
    perm = token_of_row(rows, (rows, rows), 0) == place
    first = jnp.sum(jnp.where(perm, ids[0:1, :], 0), axis=1, keepdims=True)
    second = jnp.sum(jnp.where(perm, ids[1:2, :], 0), axis=1, keepdims=True)
    logits = row_dots(x, gate)
    columns = lax.broadcasted_iota(jnp.int32, logits.shape, 1)
    l0 = jnp.sum(jnp.where(first == columns, logits, 0.0), axis=1, keepdims=True)
    l1 = jnp.sum(jnp.where(second == columns, logits, 0.0), axis=1, keepdims=True)
    return perm, first, second, jax.nn.sigmoid(l0 - l1), jax.nn.sigmoid(l1 - l0)


def forward_kernel(ids, gate, mine, other, w_up, down_t, x, gs, hidden, dpre, terms):
    rows, width = x.shape
    half = rows // 2
    expert = 2 * lax.axis_index("ey") + lax.axis_index("core")
    x[:half, :] = mine[:, 0, :]
    x[half:, :] = other[:, 0, :]
    perm, first, second, p0, p1 = gate_values(ids, gate, x)
    is0 = first == expert
    is1 = second == expert
    weight = jnp.where(is0, p0, 0.0) + jnp.where(is1, p1, 0.0)
    gs[:half, :] = (weight[:half] * mine[:, 1, :].astype(F32)).astype(BF16)
    gs[half:, :] = (weight[half:] * other[:, 1, :].astype(F32)).astype(BF16)
    pre = dot(x[...], w_up[...])
    back = dot(gs[...], down_t[...])
    sig = jax.nn.sigmoid(pre)
    silu = pre * sig
    hidden[...] = silu.astype(BF16)
    dpre[...] = (back * sig * (1.0 + pre * (1.0 - sig))).astype(BF16)
    q = jnp.sum(silu * back, axis=1, keepdims=True)
    dl = (jnp.where(is0, p1, 0.0) - jnp.where(is1, p0, 0.0)) * q
    line = jnp.sum(jnp.where(perm, dl, 0.0), axis=0, keepdims=True)
    terms[...] = jnp.broadcast_to(line[None], terms.shape)


def forward(ids, gate, mine, other, w_up, down_t):
    rows = 2 * mine.shape[0]
    width, ff = w_up.shape
    return pl.pallas_call(
        forward_kernel,
        out_shape=(
            pltpu.VMEM((rows, width), BF16),
            pltpu.VMEM((rows, width), BF16),
            pltpu.VMEM((rows, ff), BF16),
            pltpu.VMEM((rows, ff), BF16),
            pltpu.VMEM((rows, 1, rows), F32),
        ),
        in_specs=[VM] * 6,
        out_specs=(VM,) * 5,
        compiler_params=pltpu.CompilerParams(vmem_limit_bytes=16 * MIB),
        name="forward",
    )(ids, gate, mine, other, w_up, down_t)


def grads_kernel(
    chunks, x, gs, hidden, dpre, up_out, down_out, ordered, up_buf, down_buf, sems
):
    rows, width = x.shape
    ff = hidden.shape[1]
    kc, fc = width // chunks, ff // chunks
    copies = []
    for i in range(chunks):
        part = slice(i * fc, (i + 1) * fc)
        down_buf[part, :] = dot(hidden[:, part], gs[...], 0, 0).astype(BF16)
        copies.append(pltpu.make_async_copy(down_buf.at[part], down_out.at[part], sems.at[0, i]))
        copies[-1].start()
        part = slice(i * kc, (i + 1) * kc)
        up_buf[part, :] = dot(x[:, part], dpre[...], 0, 0).astype(BF16)
        copies.append(pltpu.make_async_copy(up_buf.at[part], up_out.at[part], sems.at[1, i]))
        copies[-1].start()
    perm = token_of_row(rows, (rows, rows), 1) == lax.broadcasted_iota(jnp.int32, (rows, rows), 0)
    ordered[...] = dot(perm.astype(F32).astype(BF16), x[...]).astype(BF16)
    for c in copies:
        c.wait()


def grads(x, gs, hidden, dpre):
    rows, width = x.shape
    ff = hidden.shape[1]
    chunks = 8 if ff % 1024 == 0 else 1
    return pl.pallas_call(
        functools.partial(grads_kernel, chunks),
        out_shape=(
            jax.ShapeDtypeStruct((width, ff), BF16),
            jax.ShapeDtypeStruct((ff, width), BF16),
            pltpu.VMEM((rows, width), BF16),
        ),
        in_specs=[VM] * 4,
        out_specs=(HBM, HBM, VM),
        scratch_shapes=[
            pltpu.VMEM((width, ff), BF16),
            pltpu.VMEM((ff, width), BF16),
            pltpu.SemaphoreType.DMA((2, chunks)),
        ],
        compiler_params=pltpu.CompilerParams(vmem_limit_bytes=40 * MIB),
        name="grads",
    )(x, gs, hidden, dpre)


def router_kernel(ids, x, terms, router_out):
    rows = x.shape[0]
    dl = jnp.sum(terms[...], axis=0)
    experts = router_out.shape[0]
    expert = lax.broadcasted_iota(jnp.int32, (experts, rows), 0)
    dlogit = jnp.where(ids[0:1, :] == expert, dl, 0.0) - jnp.where(ids[1:2, :] == expert, dl, 0.0)
    high = dlogit.astype(BF16)
    rest = dlogit - high.astype(F32)
    mid = rest.astype(BF16)
    low = (rest - mid.astype(F32)).astype(BF16)
    s = dot(jnp.concatenate([low, mid, high], axis=0), x[...])
    router_out[...] = s[:experts] + s[experts : 2 * experts] + s[2 * experts :]


def router(ids, x, terms, experts):
    return pl.pallas_call(
        router_kernel,
        out_shape=jax.ShapeDtypeStruct((experts, x.shape[1]), F32),
        in_specs=[VM] * 3,
        out_specs=VM,
        compiler_params=pltpu.CompilerParams(vmem_limit_bytes=16 * MIB),
        name="router",
    )(ids, x, terms)


def local(tokens, cotangent, route_ids, w_router, w_up, down_weight):
    n = lax.axis_size("dp") * lax.axis_size("ey") * 2
    rows = pack(tokens, cotangent)
    held = []
    for i, (shift, count) in enumerate(stages(n)):
        rows = spread(rows, n, shift, count)
        if i == 0:
            held = prefetch([down_weight[0]])
        elif i == 1:
            held = prefetch([w_up[0], route_ids.T, w_router], held[0])
        rows, *held = lax.optimization_barrier((rows, *held))
    other = lax.ppermute(rows, "core", [(0, 1), (1, 0)])
    down_t, up, ids, gate = held
    x, gs, hidden, dpre, terms = forward(ids, gate, rows, other, up, down_t)
    terms = lax.all_to_all(terms, AXES, 0, 0, tiled=True)
    grad_up, grad_down, ordered = grads(x, gs, hidden, dpre)
    grad_router = router(ids, ordered, terms, w_router.shape[0])
    return (grad_up[None], grad_down[None], grad_router)


def solution(mesh):
    n_data, n_experts = mesh.shape["dp"], mesh.shape["expert"]
    split = Mesh(mesh.devices.reshape(n_data, n_experts // 2, 2), AXES)
    experts = ("ey", "core")
    return jax.shard_map(
        local,
        mesh=split,
        in_specs=(
            P(AXES, None),
            P(AXES, None),
            P(),
            P(),
            P(experts, None, "dp"),
            P(experts, "dp", None),
        ),
        out_specs=(P(experts, None, "dp"), P(experts, "dp", None), P()),
        check_vma=False,
    )
```

```python
import functools

import jax
import jax.numpy as jnp
from jax import lax
from jax.experimental import pallas as pl
from jax.experimental.pallas import tpu as pltpu
from jax.sharding import Mesh, PartitionSpec as P

F32 = jnp.float32
BF16 = jnp.bfloat16
CHIPS = ("dp", "ey")
AXES = ("dp", "ey", "core")
MIB = 1024 * 1024
VM = pl.BlockSpec(memory_space=pltpu.VMEM)
HBM = pl.BlockSpec(memory_space=pltpu.HBM)


def dot(a, b, ca=1, cb=0):
    return lax.dot_general(a, b, (((ca,), (cb,)), ((), ())), preferred_element_type=F32)


def in_hbm(x):
    return pltpu.with_memory_space_constraint(x, pltpu.HBM)


def pack_kernel(tokens, cotangent, out, buf, sems):
    loads = [
        pltpu.make_async_copy(ref, buf.at[i], sems.at[i]) for i, ref in enumerate((tokens, cotangent))
    ]
    for c in loads:
        c.start()
    for c in loads:
        c.wait()
    out[...] = jnp.concatenate([buf[0], buf[1]], axis=0)[None]


def pack(tokens, cotangent):
    return pl.pallas_call(
        pack_kernel,
        out_shape=pltpu.VMEM((1, 2, tokens.shape[1]), BF16),
        in_specs=[HBM, HBM],
        out_specs=VM,
        scratch_shapes=[pltpu.VMEM((2,) + tokens.shape, BF16), pltpu.SemaphoreType.DMA((2,))],
        compiler_params=pltpu.CompilerParams(vmem_limit_bytes=16 * MIB),
        name="pack",
    )(in_hbm(tokens), in_hbm(cotangent))


def stages(n):
    bits = n.bit_length() - 1
    shifts, high = [], bits
    while high > 1:
        low = max(1, high - 2)
        shifts.append((low, high - low))
        high = low
    return shifts


def spread(blocks, n, shift, count):
    parts = [blocks]
    for step in range(1, 1 << count):
        pairs = [(i, i ^ (step << shift)) for i in range(n)]
        parts.append(lax.ppermute(blocks, AXES, pairs))
    return jnp.concatenate(parts, axis=0)


def prefetch_kernel(count, *refs):
    sources, targets, sems = refs[:count], refs[-1 - count : -1], refs[-1]
    copies = [
        pltpu.make_async_copy(source, target, sems.at[i])
        for i, (source, target) in enumerate(zip(sources, targets))
    ]
    for c in copies:
        c.start()
    if len(refs) > 2 * count + 1:
        held, turned = refs[count], refs[count + 1]
        step = min(256, held.shape[0])
        for i in range(0, held.shape[0], step):
            turned[:, i : i + step] = held[i : i + step, :].T
    for c in copies:
        c.wait()


def prefetch(arrays, held=None):
    extra = [] if held is None else [held]
    turned = [pltpu.VMEM(h.shape[::-1], h.dtype) for h in extra]
    return pl.pallas_call(
        functools.partial(prefetch_kernel, len(arrays)),
        out_shape=tuple(turned) + tuple(pltpu.VMEM(a.shape, a.dtype) for a in arrays),
        in_specs=[HBM] * len(arrays) + [VM] * len(extra),
        out_specs=(VM,) * (len(arrays) + len(extra)),
        scratch_shapes=[pltpu.SemaphoreType.DMA((len(arrays),))],
        compiler_params=pltpu.CompilerParams(vmem_limit_bytes=8 * MIB),
        name="turn" if extra else "prefetch",
    )(*[in_hbm(a) for a in arrays], *extra)


def device_index():
    place = lax.axis_index("dp") * lax.axis_size("ey") + lax.axis_index("ey")
    return 2 * place + lax.axis_index("core")


def token_of_row(rows, shape, dim):
    row = lax.broadcasted_iota(jnp.int32, shape, dim)
    half = rows // 2
    token = jnp.where(row < half, 0, 1) ^ device_index()
    digits = lax.rem(row, half)
    for shift, count in stages(rows):
        token = token ^ ((digits & ((1 << count) - 1)) << shift)
        digits = digits >> count
    return token


def gate_values(ids, gate, x):
    rows = x.shape[0]
    place = lax.broadcasted_iota(jnp.int32, (rows, rows), 1)
    perm = token_of_row(rows, (rows, rows), 0) == place
    first = jnp.sum(jnp.where(perm, ids[0:1, :], 0), axis=1, keepdims=True)
    second = jnp.sum(jnp.where(perm, ids[1:2, :], 0), axis=1, keepdims=True)
    logits = dot(x[...], gate[...], 1, 1)
    columns = lax.broadcasted_iota(jnp.int32, logits.shape, 1)
    l0 = jnp.sum(jnp.where(first == columns, logits, 0.0), axis=1, keepdims=True)
    l1 = jnp.sum(jnp.where(second == columns, logits, 0.0), axis=1, keepdims=True)
    return perm, first, second, jax.nn.sigmoid(l0 - l1), jax.nn.sigmoid(l1 - l0)


def forward_kernel(ids, gate, mine, other, w_up, down_t, x, gs, hidden, dpre, terms):
    rows, width = x.shape
    expert = 2 * lax.axis_index("ey") + lax.axis_index("core")
    pre = jnp.zeros((rows, w_up.shape[1]), F32)
    back = jnp.zeros((rows, w_up.shape[1]), F32)
    step = min(256, width)
    for k in range(0, width, step):
        part = slice(k, k + step)
        x[:, part] = jnp.concatenate([mine[:, 0, part], other[:, 0, part]], axis=0)
        g = jnp.concatenate([mine[:, 1, part], other[:, 1, part]], axis=0)
        pre = pre + dot(x[:, part], w_up[part, :])
        gs[:, part] = g
        back = back + dot(g, down_t[part, :])
    perm, first, second, p0, p1 = gate_values(ids, gate, x)
    is0 = first == expert
    is1 = second == expert
    weight = jnp.where(is0, p0, 0.0) + jnp.where(is1, p1, 0.0)
    back = weight * back
    gs[...] = (weight * gs[...].astype(F32)).astype(BF16)
    sig = jax.nn.sigmoid(pre)
    silu = pre * sig
    hidden[...] = silu.astype(BF16)
    dpre[...] = (back * sig * (1.0 + pre * (1.0 - sig))).astype(BF16)
    q = jnp.sum(silu * back, axis=1, keepdims=True)
    dl = (jnp.where(is0, p1, 0.0) - jnp.where(is1, p0, 0.0)) * q
    line = jnp.sum(jnp.where(perm, dl, 0.0), axis=0, keepdims=True)
    terms[...] = jnp.broadcast_to(line[None], terms.shape)


def forward(ids, gate, mine, other, w_up, down_t):
    rows = 2 * mine.shape[0]
    width, ff = w_up.shape
    return pl.pallas_call(
        forward_kernel,
        out_shape=(
            pltpu.VMEM((rows, width), BF16),
            pltpu.VMEM((rows, width), BF16),
            pltpu.VMEM((rows, ff), BF16),
            pltpu.VMEM((rows, ff), BF16),
            pltpu.VMEM((rows, 1, rows), F32),
        ),
        in_specs=[VM] * 6,
        out_specs=(VM,) * 5,
        compiler_params=pltpu.CompilerParams(vmem_limit_bytes=16 * MIB),
        name="forward",
    )(ids, gate, mine, other, w_up, down_t)


def grads_kernel(
    chunks, x, gs, hidden, dpre, up_out, down_out, ordered, up_buf, down_buf, sems
):
    rows, width = x.shape
    ff = hidden.shape[1]
    kc, fc = width // chunks, ff // chunks
    copies = []
    for i in range(chunks):
        part = slice(i * fc, (i + 1) * fc)
        down_buf[part, :] = dot(hidden[:, part], gs[...], 0, 0).astype(BF16)
        copies.append(pltpu.make_async_copy(down_buf.at[part], down_out.at[part], sems.at[0, i]))
        copies[-1].start()
        part = slice(i * kc, (i + 1) * kc)
        up_buf[part, :] = dot(x[:, part], dpre[...], 0, 0).astype(BF16)
        copies.append(pltpu.make_async_copy(up_buf.at[part], up_out.at[part], sems.at[1, i]))
        copies[-1].start()
    perm = token_of_row(rows, (rows, rows), 1) == lax.broadcasted_iota(jnp.int32, (rows, rows), 0)
    ordered[...] = dot(perm.astype(F32).astype(BF16), x[...]).astype(BF16)
    for c in copies:
        c.wait()


def grads(x, gs, hidden, dpre):
    rows, width = x.shape
    ff = hidden.shape[1]
    chunks = 8 if ff % 1024 == 0 else 1
    return pl.pallas_call(
        functools.partial(grads_kernel, chunks),
        out_shape=(
            jax.ShapeDtypeStruct((width, ff), BF16),
            jax.ShapeDtypeStruct((ff, width), BF16),
            pltpu.VMEM((rows, width), BF16),
        ),
        in_specs=[VM] * 4,
        out_specs=(HBM, HBM, VM),
        scratch_shapes=[
            pltpu.VMEM((width, ff), BF16),
            pltpu.VMEM((ff, width), BF16),
            pltpu.SemaphoreType.DMA((2, chunks)),
        ],
        compiler_params=pltpu.CompilerParams(vmem_limit_bytes=40 * MIB),
        name="grads",
    )(x, gs, hidden, dpre)


def router_kernel(ids, x, terms, router_out):
    rows = x.shape[0]
    dl = jnp.sum(terms[...], axis=0)
    experts = router_out.shape[0]
    expert = lax.broadcasted_iota(jnp.int32, (experts, rows), 0)
    dlogit = jnp.where(ids[0:1, :] == expert, dl, 0.0) - jnp.where(ids[1:2, :] == expert, dl, 0.0)
    high = dlogit.astype(BF16)
    rest = dlogit - high.astype(F32)
    mid = rest.astype(BF16)
    low = (rest - mid.astype(F32)).astype(BF16)
    s = dot(jnp.concatenate([low, mid, high], axis=0), x[...])
    router_out[...] = s[:experts] + s[experts : 2 * experts] + s[2 * experts :]


def router(ids, x, terms, experts):
    return pl.pallas_call(
        router_kernel,
        out_shape=jax.ShapeDtypeStruct((experts, x.shape[1]), F32),
        in_specs=[VM] * 3,
        out_specs=VM,
        compiler_params=pltpu.CompilerParams(vmem_limit_bytes=16 * MIB),
        name="router",
    )(ids, x, terms)


def local(tokens, cotangent, route_ids, w_router, w_up, down_weight):
    n = lax.axis_size("dp") * lax.axis_size("ey") * 2
    rows = pack(tokens, cotangent)
    held = []
    for i, (shift, count) in enumerate(stages(n)):
        rows = spread(rows, n, shift, count)
        if i == 0:
            held = prefetch([down_weight[0]])
        elif i == 1:
            held = prefetch([w_up[0], route_ids.T, w_router], held[0])
        rows, *held = lax.optimization_barrier((rows, *held))
    other = lax.ppermute(rows, "core", [(0, 1), (1, 0)])
    down_t, up, ids, gate = held
    x, gs, hidden, dpre, terms = forward(ids, gate, rows, other, up, down_t)
    terms = lax.all_to_all(terms, AXES, 0, 0, tiled=True)
    grad_up, grad_down, ordered = grads(x, gs, hidden, dpre)
    grad_router = router(ids, ordered, terms, w_router.shape[0])
    return (grad_up[None], grad_down[None], grad_router)


def solution(mesh):
    n_data, n_experts = mesh.shape["dp"], mesh.shape["expert"]
    split = Mesh(mesh.devices.reshape(n_data, n_experts // 2, 2), AXES)
    experts = ("ey", "core")
    return jax.shard_map(
        local,
        mesh=split,
        in_specs=(
            P(AXES, None),
            P(AXES, None),
            P(),
            P(),
            P(experts, None, "dp"),
            P(experts, "dp", None),
        ),
        out_specs=(P(experts, None, "dp"), P(experts, "dp", None), P()),
        check_vma=False,
    )
```

```python
import functools

import jax
import jax.numpy as jnp
from jax import lax
from jax.experimental import pallas as pl
from jax.experimental.pallas import tpu as pltpu
from jax.sharding import Mesh, PartitionSpec as P

F32 = jnp.float32
BF16 = jnp.bfloat16
CHIPS = ("dp", "ey")
AXES = ("dp", "ey", "core")
MIB = 1024 * 1024
VM = pl.BlockSpec(memory_space=pltpu.VMEM)
HBM = pl.BlockSpec(memory_space=pltpu.HBM)


def dot(a, b, ca=1, cb=0):
    return lax.dot_general(a, b, (((ca,), (cb,)), ((), ())), preferred_element_type=F32)


def in_hbm(x):
    return pltpu.with_memory_space_constraint(x, pltpu.HBM)


def pack_kernel(tokens, cotangent, out, buf, sems):
    loads = [
        pltpu.make_async_copy(ref, buf.at[i], sems.at[i]) for i, ref in enumerate((tokens, cotangent))
    ]
    for c in loads:
        c.start()
    for c in loads:
        c.wait()
    out[...] = jnp.concatenate([buf[0], buf[1]], axis=0)[None]


def pack(tokens, cotangent):
    return pl.pallas_call(
        pack_kernel,
        out_shape=pltpu.VMEM((1, 2, tokens.shape[1]), BF16),
        in_specs=[HBM, HBM],
        out_specs=VM,
        scratch_shapes=[pltpu.VMEM((2,) + tokens.shape, BF16), pltpu.SemaphoreType.DMA((2,))],
        compiler_params=pltpu.CompilerParams(vmem_limit_bytes=16 * MIB),
        name="pack",
    )(in_hbm(tokens), in_hbm(cotangent))


def stages(n):
    bits = n.bit_length() - 1
    shifts, high = [], bits
    while high > 1:
        low = max(1, high - 2)
        shifts.append((low, high - low))
        high = low
    return shifts


def spread(blocks, n, shift, count):
    parts = [blocks]
    for step in range((1 << count) - 1, 0, -1):
        pairs = [(i, i ^ (step << shift)) for i in range(n)]
        parts.append(lax.ppermute(blocks, AXES, pairs))
    return jnp.concatenate(parts, axis=0)


def prefetch_kernel(count, spans, *refs):
    sources, targets, sems = refs[:count], refs[-1 - count : -1], refs[-1]
    copies = [
        pltpu.make_async_copy(source if span is None else source.at[pl.ds(*span)], target, sems.at[i])
        for i, (source, span, target) in enumerate(zip(sources, spans, targets))
    ]
    for c in copies:
        c.start()
    if len(refs) > 2 * count + 1:
        held, turned = refs[count], refs[count + 1]
        step = min(256, held.shape[0])
        for i in range(0, held.shape[0], step):
            turned[:, i : i + step] = held[i : i + step, :].T
    for c in copies:
        c.wait()


def prefetch(arrays, held=None, span=None):
    extra = [] if held is None else [held]
    spans = [span] + [None] * (len(arrays) - 1)
    shapes = [a.shape if p is None else (p[1],) + a.shape[1:] for a, p in zip(arrays, spans)]
    turned = [pltpu.VMEM(h.shape[::-1], h.dtype) for h in extra]
    return pl.pallas_call(
        functools.partial(prefetch_kernel, len(arrays), spans),
        out_shape=tuple(turned) + tuple(pltpu.VMEM(p, a.dtype) for a, p in zip(arrays, shapes)),
        in_specs=[HBM] * len(arrays) + [VM] * len(extra),
        out_specs=(VM,) * (len(arrays) + len(extra)),
        scratch_shapes=[pltpu.SemaphoreType.DMA((len(arrays),))],
        compiler_params=pltpu.CompilerParams(vmem_limit_bytes=8 * MIB),
        name="turn" if extra else "prefetch",
    )(*[in_hbm(a) for a in arrays], *extra)


def device_index():
    place = lax.axis_index("dp") * lax.axis_size("ey") + lax.axis_index("ey")
    return 2 * place + lax.axis_index("core")


def token_of_row(rows, shape, dim):
    row = lax.broadcasted_iota(jnp.int32, shape, dim)
    half = rows // 2
    token = jnp.where(row < half, 0, 1) ^ device_index()
    digits = lax.rem(row, half)
    for shift, count in stages(rows):
        token = token ^ ((-digits & ((1 << count) - 1)) << shift)
        digits = digits >> count
    return token


def gate_values(ids, gate, x):
    rows = x.shape[0]
    place = lax.broadcasted_iota(jnp.int32, (rows, rows), 1)
    perm = token_of_row(rows, (rows, rows), 0) == place
    first = jnp.sum(jnp.where(perm, ids[0:1, :], 0), axis=1, keepdims=True)
    second = jnp.sum(jnp.where(perm, ids[1:2, :], 0), axis=1, keepdims=True)
    logits = dot(x[...], gate[...], 1, 1)
    columns = lax.broadcasted_iota(jnp.int32, logits.shape, 1)
    l0 = jnp.sum(jnp.where(first == columns, logits, 0.0), axis=1, keepdims=True)
    l1 = jnp.sum(jnp.where(second == columns, logits, 0.0), axis=1, keepdims=True)
    return perm, first, second, jax.nn.sigmoid(l0 - l1), jax.nn.sigmoid(l1 - l0)


def forward_kernel(
    ids, gate, mine, other, up_head, up_tail, down_t, x, gs, hidden, dpre, terms_out, terms, sem
):
    rows, width = x.shape
    expert = 2 * lax.axis_index("ey") + lax.axis_index("core")
    head = up_head.shape[0]
    pre = jnp.zeros((rows, down_t.shape[1]), F32)
    back = jnp.zeros((rows, down_t.shape[1]), F32)
    step = min(256, width)
    for k in range(0, width, step):
        part = slice(k, k + step)
        x[:, part] = jnp.concatenate([mine[:, 0, part], other[:, 0, part]], axis=0)
        g = jnp.concatenate([mine[:, 1, part], other[:, 1, part]], axis=0)
        w_up = up_head[part, :] if k < head else up_tail[k - head : k - head + step, :]
        pre = pre + dot(x[:, part], w_up)
        gs[:, part] = g
        back = back + dot(g, down_t[part, :])
    perm, first, second, p0, p1 = gate_values(ids, gate, x)
    is0 = first == expert
    is1 = second == expert
    weight = jnp.where(is0, p0, 0.0) + jnp.where(is1, p1, 0.0)
    back = weight * back
    sig = jax.nn.sigmoid(pre)
    silu = pre * sig
    q = jnp.sum(silu * back, axis=1, keepdims=True)
    dl = (jnp.where(is0, p1, 0.0) - jnp.where(is1, p0, 0.0)) * q
    line = jnp.sum(jnp.where(perm, dl, 0.0), axis=0, keepdims=True)
    terms[...] = jnp.broadcast_to(line[None], terms.shape)
    copy = pltpu.make_async_copy(terms, terms_out, sem)
    copy.start()
    gs[...] = (weight * gs[...].astype(F32)).astype(BF16)
    hidden[...] = silu.astype(BF16)
    dpre[...] = (back * sig * (1.0 + pre * (1.0 - sig))).astype(BF16)
    copy.wait()


def forward(ids, gate, mine, other, up_head, up_tail, down_t):
    rows = 2 * mine.shape[0]
    width, ff = down_t.shape
    return pl.pallas_call(
        forward_kernel,
        out_shape=(
            pltpu.VMEM((rows, width), BF16),
            pltpu.VMEM((rows, width), BF16),
            pltpu.VMEM((rows, ff), BF16),
            pltpu.VMEM((rows, ff), BF16),
            pltpu.HBM((rows, 1, rows), F32),
        ),
        in_specs=[VM] * 7,
        out_specs=(VM,) * 4 + (HBM,),
        scratch_shapes=[pltpu.VMEM((rows, 1, rows), F32), pltpu.SemaphoreType.DMA],
        compiler_params=pltpu.CompilerParams(vmem_limit_bytes=16 * MIB),
        name="forward",
    )(ids, gate, mine, other, up_head, up_tail, down_t)


def grads_kernel(
    chunks, x, gs, hidden, dpre, up_out, down_out, ordered, up_buf, down_buf, sems
):
    rows, width = x.shape
    ff = hidden.shape[1]
    kc, fc = width // chunks, ff // chunks
    copies = []
    for i in range(chunks):
        part = slice(i * fc, (i + 1) * fc)
        down_buf[part, :] = dot(hidden[:, part], gs[...], 0, 0).astype(BF16)
        copies.append(pltpu.make_async_copy(down_buf.at[part], down_out.at[part], sems.at[0, i]))
        copies[-1].start()
        part = slice(i * kc, (i + 1) * kc)
        up_buf[part, :] = dot(x[:, part], dpre[...], 0, 0).astype(BF16)
        copies.append(pltpu.make_async_copy(up_buf.at[part], up_out.at[part], sems.at[1, i]))
        copies[-1].start()
    perm = token_of_row(rows, (rows, rows), 1) == lax.broadcasted_iota(jnp.int32, (rows, rows), 0)
    ordered[...] = dot(perm.astype(F32).astype(BF16), x[...]).astype(BF16)
    for c in copies:
        c.wait()


def grads(x, gs, hidden, dpre):
    rows, width = x.shape
    ff = hidden.shape[1]
    chunks = 8 if ff % 1024 == 0 else 1
    return pl.pallas_call(
        functools.partial(grads_kernel, chunks),
        out_shape=(
            jax.ShapeDtypeStruct((width, ff), BF16),
            jax.ShapeDtypeStruct((ff, width), BF16),
            pltpu.VMEM((rows, width), BF16),
        ),
        in_specs=[VM] * 4,
        out_specs=(HBM, HBM, VM),
        scratch_shapes=[
            pltpu.VMEM((width, ff), BF16),
            pltpu.VMEM((ff, width), BF16),
            pltpu.SemaphoreType.DMA((2, chunks)),
        ],
        compiler_params=pltpu.CompilerParams(vmem_limit_bytes=40 * MIB),
        name="grads",
    )(x, gs, hidden, dpre)


def router_kernel(ids, x, terms, router_out):
    rows = x.shape[0]
    dl = jnp.sum(terms[...], axis=0)
    experts = router_out.shape[0]
    expert = lax.broadcasted_iota(jnp.int32, (experts, rows), 0)
    dlogit = jnp.where(ids[0:1, :] == expert, dl, 0.0) - jnp.where(ids[1:2, :] == expert, dl, 0.0)
    high = dlogit.astype(BF16)
    rest = dlogit - high.astype(F32)
    mid = rest.astype(BF16)
    low = (rest - mid.astype(F32)).astype(BF16)
    s = dot(jnp.concatenate([low, mid, high], axis=0), x[...])
    router_out[...] = s[:experts] + s[experts : 2 * experts] + s[2 * experts :]


def router(ids, x, terms, experts):
    return pl.pallas_call(
        router_kernel,
        out_shape=jax.ShapeDtypeStruct((experts, x.shape[1]), F32),
        in_specs=[VM] * 3,
        out_specs=VM,
        compiler_params=pltpu.CompilerParams(vmem_limit_bytes=16 * MIB),
        name="router",
    )(ids, x, terms)


def local(tokens, cotangent, route_ids, w_router, w_up, down_weight):
    n = lax.axis_size("dp") * lax.axis_size("ey") * 2
    rows = pack(tokens, cotangent)
    width = tokens.shape[1]
    head = 3 * width // 4
    held = []
    for i, (shift, count) in enumerate(stages(n)):
        rows = spread(rows, n, shift, count)
        if i == 0:
            held = prefetch([down_weight[0]])
        elif i == 1:
            held = prefetch([w_up[0], route_ids.T, w_router], held[0], (0, head))
        rows, *held = lax.optimization_barrier((rows, *held))
    other = lax.ppermute(rows, "core", [(0, 1), (1, 0)])
    down_t, up, ids, gate = held
    (tail,) = prefetch([w_up[0]], None, (head, width - head))
    x, gs, hidden, dpre, terms = forward(ids, gate, rows, other, up, tail, down_t)
    terms = lax.all_to_all(terms, AXES, 0, 0, tiled=True)
    grad_up, grad_down, ordered = grads(x, gs, hidden, dpre)
    grad_router = router(ids, ordered, terms, w_router.shape[0])
    return (grad_up[None], grad_down[None], grad_router)


def solution(mesh):
    n_data, n_experts = mesh.shape["dp"], mesh.shape["expert"]
    split = Mesh(mesh.devices.reshape(n_data, n_experts // 2, 2), AXES)
    experts = ("ey", "core")
    return jax.shard_map(
        local,
        mesh=split,
        in_specs=(
            P(AXES, None),
            P(AXES, None),
            P(),
            P(),
            P(experts, None, "dp"),
            P(experts, "dp", None),
        ),
        out_specs=(P(experts, None, "dp"), P(experts, "dp", None), P()),
        check_vma=False,
    )
```
